512 devices in a mesh: dp: 64 (over z, x_lo, core), mp: 8 (over y, x_hi).
Axes of the slice: x: 4 (x_hi: 2, x_lo: 2; x = x_hi * 2 + x_lo), y: 4, z: 16, core: 2. Of those that a mesh axis runs over, the one named last changes fastest.
Arguments:
- latents: bfloat16 [512, 512, 1024], P('dp', None, 'mp'), may hold values from -16 to 16
- labels: bfloat16 [512, 512, 128], P('dp'), may hold values from -6 to 6
- slot_source: int32 [128], replicated, may hold values from 0 to 127, each once
- episode_pick: int32 [128], replicated, may hold values from 0 to 7
- window_start: int32 [128], replicated, may hold values from 0 to 256
- proj_weight: bfloat16 [1024, 6144], P('dp', 'mp')
- norm_gain: float32 [6144], P('mp'), may hold values from 0.25 to 1.75
- head_weight: bfloat16 [6144, 128], P('mp'), may hold values from -0.078125 to 0.078125
Outputs:
- grad_proj: float32 [1024, 6144], P('dp', 'mp')
- grad_head: float32 [6144, 128], P('mp')
- grad_gain: float32 [6144], P('mp')
- features: bfloat16 [32768, 6144], P('dp', 'mp')
The draws below stay inside these ranges and needn't reach their ends.
Inputs may be any that keep to these rules, and one draw needn't show every extreme that they name: slot_source is a permutation of 0 to 127, so each shard of 8 episodes fills exactly 2 batch windows.
All inputs are finite; a program needn't handle non-finite values.
Results may differ from the reference program's by a relative error of at most 0.0065.
Values may be sent and summed in bfloat16 or wider, within the bound.
No kernel may reach another device: no remote copies, remote signals or barrier semaphores. Data moves between devices by JAX's collectives and lax.ppermute only.
A program may use at most 64 MiB of HBM per device.

```python
import math
import jax
import jax.numpy as jnp
from jax import lax

D = 6144
LAT = 1024
ACT = 128
WIN = 256
STEPS = 512
EP_DEV = 8
SLOTS_DEV = 2
SLOTS = 128
TOKENS = 32768
EPISODES = 512
N_DP = 64


def draw_proj_weight(key, part):
    key = jax.random.fold_in(key, 11)
    entry_key, spread_key = jax.random.split(key)
    columns = jnp.arange(D, dtype=jnp.float32)
    column_ramp = jnp.exp(math.log(3.0) * (columns / (D - 1) - 0.5))
    entries = jax.random.normal(entry_key, (LAT, D), jnp.float32)
    spread = jnp.exp(jax.random.uniform(spread_key, (D,), jnp.float32, math.log(0.3), math.log(3.0)))
    return (entries * (spread * column_ramp) * LAT ** (-0.5)).astype(jnp.bfloat16)


def draw_window_start(key, part):
    key = jax.random.fold_in(key, 23)
    start_key, place_key = jax.random.split(key)
    starts = jax.random.randint(start_key, (SLOTS,), 0, STEPS - WIN + 1, dtype=jnp.int32)
    chosen = jax.random.randint(place_key, (), 0, SLOTS, dtype=jnp.int32)
    return jnp.where(jnp.arange(SLOTS, dtype=jnp.int32) == chosen, STEPS - WIN, starts).astype(jnp.int32)


def plant(result, key, low, high):
    extent = result.shape
    place = [jax.random.randint(jax.random.fold_in(key, axis), (), 0, extent[axis]) for axis in range(len(extent))]
    result = result.at[tuple(place)].set(low)
    longest = extent.index(max(extent))
    place[longest] = (place[longest] + 1) % extent[longest]
    return result.at[tuple(place)].set(high)


def strengthened(values, stream_key, source, target, shards_of, factor):
    def block_of(axis_at):
        return (jnp.arange(values.shape[axis_at]) // (values.shape[axis_at] // shards_of)).reshape((-1,) + (1,) * (values.ndim - 1 - axis_at))

    one_side = jax.random.permutation(stream_key, shards_of)[block_of(target)]
    far = (block_of(target) + shards_of // 2) % shards_of
    return jnp.where((block_of(source) == one_side) | (block_of(source) == far), factor * values, values)


def shard_levels(stream_key, extent, pieces, least, top_value):
    gain, own = 1.0, jax.random.fold_in(stream_key, 6)
    for axis_at, blocks in pieces:
        steps = jnp.exp(jax.random.uniform(jax.random.fold_in(own, axis_at), (blocks,), jnp.float32, least / len(pieces), top_value / len(pieces)))
        gain = gain * jnp.repeat(steps, extent[axis_at] // blocks).reshape([-1 if axis == axis_at else 1 for axis in range(len(extent))])
    return gain


def noise(own_key, shape, deviation, reach, pieces=(), held_as=jnp.bfloat16):
    array = jax.random.normal(own_key, shape, jnp.float32) * deviation
    if len(pieces) > 0:
        array = shard_levels(own_key, shape, pieces, -0.22, 0.18) * array
    return jnp.clip(array, min=-reach, max=reach).astype(held_as)


def gaussian_with(key, dims, deviation, limit, pieces, heavy, held_as=jnp.bfloat16):
    values = deviation * jax.random.normal(key, dims, jnp.float32)
    if pieces:
        values = values * shard_levels(key, dims, pieces, -0.22, 0.18)
    return jnp.clip(strengthened(values, jax.random.fold_in(key, 3), *heavy), -limit, limit).astype(held_as)


def setup_inputs(seed: int = 0) -> dict:
    splits = jax.random.split(jax.random.key(seed), 9)
    return {
        "latents": gaussian_with(splits[0], (EPISODES, STEPS, LAT), 1.0, 16.0, ((0, 64), (2, 8)), (0, 2, 64, 4.0)),
        "labels": noise(splits[1], (EPISODES, STEPS, ACT), 1.0, 6.0, ((0, 64),)),
        "slot_source": jax.random.permutation(splits[2], SLOTS).astype(jnp.int32),
        "episode_pick": plant(jax.random.randint(splits[3], (SLOTS,), 0, EP_DEV), jax.random.fold_in(splits[3], 1), 0, EP_DEV - 1).astype(jnp.int32),
        "window_start": draw_window_start(jax.random.fold_in(splits[8], 71), 0),
        "proj_weight": draw_proj_weight(jax.random.fold_in(splits[8], 71), 0),
        "norm_gain": jnp.clip(1.0 + 0.15 * jax.random.normal(splits[6], (D,), jnp.float32), 0.25, 1.75),
        "head_weight": noise(splits[7], (D, ACT), D ** -0.5, 0.078125, ((0, 8),)),
    }


EPSILON = 1e-05

def forward_backward(inputs, targets, proj_weight, norm_gain, head_weight):
    hidden = jnp.dot(inputs, proj_weight, preferred_element_type=jnp.float32)
    row_sum = lax.optimization_barrier(jnp.sum(hidden, axis=1))
    row_square = lax.optimization_barrier(jnp.sum(hidden * hidden, axis=1))
    row_mean = row_sum / D
    variance = row_square / D - row_mean * row_mean
    row_scale = lax.rsqrt(variance + EPSILON)
    normed = (hidden - row_mean[:, None]) * row_scale[:, None]
    features = (normed * norm_gain).astype(jnp.bfloat16)
    predicted = jnp.dot(features, head_weight, preferred_element_type=jnp.float32)
    error_grad = ((predicted - targets.astype(jnp.float32)) / math.sqrt(TOKENS)).astype(jnp.bfloat16)
    head_term = lax.dot_general(features, error_grad, (((0,), (0,)), ((), ())), preferred_element_type=jnp.float32)
    back_feat = lax.dot_general(error_grad, head_weight, (((1,), (1,)), ((), ())), preferred_element_type=jnp.float32)
    gain_term = lax.optimization_barrier(jnp.sum(back_feat * normed, axis=0))
    back_norm = back_feat * norm_gain
    first_sum = lax.optimization_barrier(jnp.sum(back_norm, axis=1))
    second_sum = lax.optimization_barrier(jnp.sum(back_norm * normed, axis=1))
    back_hidden = (row_scale[:, None] * (back_norm - first_sum[:, None] / D - normed * (second_sum[:, None] / D))).astype(jnp.bfloat16)
    proj_term = lax.dot_general(inputs, back_hidden, (((0,), (0,)), ((), ())), preferred_element_type=jnp.float32)
    return (proj_term, head_term, gain_term, features)

def reference(latents, labels, slot_source, episode_pick, window_start, proj_weight, norm_gain, head_weight):
    owner_shard = (slot_source // SLOTS_DEV).astype(jnp.int32)
    episode_index = (owner_shard * EP_DEV + episode_pick).astype(jnp.int32)
    first_steps = window_start.astype(jnp.int32)
    zero_index = jnp.zeros((), jnp.int32)

    def cut_window(episode, offset):
        window_lat = lax.dynamic_slice(latents, (episode, offset, zero_index), (1, WIN, LAT))[0]
        window_lab = lax.dynamic_slice(labels, (episode, offset, zero_index), (1, WIN, ACT))[0]
        return (window_lat, window_lab)

    def group_step(totals, group_picks):
        episodes, offsets = group_picks
        window_lat, window_lab = jax.vmap(cut_window)(episodes, offsets)
        inputs = window_lat.reshape(SLOTS_DEV * WIN, LAT)
        targets = window_lab.reshape(SLOTS_DEV * WIN, ACT)
        proj_term, head_term, gain_term, features = forward_backward(inputs, targets, proj_weight, norm_gain, head_weight)
        return ((totals[0] + proj_term, totals[1] + head_term, totals[2] + gain_term), features)
    initial = (jnp.zeros((LAT, D), jnp.float32), jnp.zeros((D, ACT), jnp.float32), jnp.zeros((D,), jnp.float32))
    totals, stacked = lax.scan(group_step, initial, (episode_index.reshape(N_DP, SLOTS_DEV), first_steps.reshape(N_DP, SLOTS_DEV)))
    return (totals[0], totals[1], totals[2], stacked.reshape(TOKENS, D))
```

```python
import math

import jax
import jax.numpy as jnp
from jax import lax
from jax.experimental import pallas as pl
from jax.experimental.pallas import tpu as pltpu
from jax.sharding import PartitionSpec as P

D = 6144
WIN = 256
EPSILON = 1e-05
BF = jnp.bfloat16
F32 = jnp.float32

N_DP = 64
Z_GROUPS = [[z * 4 + q for z in range(16)] for q in range(4)]


def to_core(i):
    return i ^ 1


def to_xlo(i):
    return i ^ 2


def to_zl(k):
    return lambda i: (i & ~12) | ((i + 4 * k) & 12)


def to_zh(k):
    return lambda i: (i + 16 * k) % N_DP


def permute(x, target):
    return lax.ppermute(x, "dp", [(i, target(i)) for i in range(N_DP)])


def exchange(x, axis, groups=None):
    return lax.all_to_all(
        x, axis, split_axis=0, concat_axis=0, tiled=True, axis_index_groups=groups
    )


def gather(x, axis, groups=None):
    return lax.all_gather(x, axis, axis=0, tiled=True, axis_index_groups=groups)


def copies(x, n):
    return jnp.broadcast_to(x[None], (n,) + x.shape)


def take(x, index, axis):
    return lax.dynamic_index_in_dim(x, index, axis, keepdims=False)


def pair(mine, other, index):
    return jnp.where(index == 0, jnp.stack([mine, other]), jnp.stack([other, mine]))


def scatter4(blocks, index, to):
    total = take(blocks, index, 0)
    for k in (1, 2, 3):
        sent = take(blocks, (index + k) % 4, 0).astype(BF)
        total = total + permute(sent, to(k)).astype(F32)
    return total


def tie(x, y):
    return lax.optimization_barrier((x, y))


def cut_kernel(
    position_ref, slot_ref, pick_ref, start_ref, latents_ref, labels_ref,
    copies_ref, own_ref, targets_ref, lat_held, lab_held, wide, sems,
):
    shifts, moves = [], []
    for k in range(2):
        here = slot_ref[...] == position_ref[0] * 2 + k
        episode = jnp.sum(jnp.where(here, pick_ref[...], 0).astype(F32)).astype(jnp.int32)
        start = jnp.sum(jnp.where(here, start_ref[...], 0).astype(F32)).astype(jnp.int32)
        first = pl.multiple_of(jnp.minimum(start // 16, 15) * 16, 16)
        shifts.append(start - first)
        for n, (store, held) in enumerate(((latents_ref, lat_held), (labels_ref, lab_held))):
            move = pltpu.make_async_copy(
                store.at[episode, pl.ds(first, WIN + 16), :], held.at[k], sems.at[n, k]
            )
            move.start()
            moves.append(move)
    for k in range(2):
        rows = slice(k * WIN, (k + 1) * WIN)
        moves[2 * k].wait()
        wide[k] = lat_held[k].astype(F32)
        window = wide[k, pl.ds(shifts[k], WIN), :].astype(BF)
        own_ref[rows, :] = window
        for m in range(8):
            copies_ref[m, rows, :] = window
    for k in range(2):
        moves[2 * k + 1].wait()
        wide[k] = lab_held[k].astype(F32)
        targets_ref[k * WIN : (k + 1) * WIN, :] = wide[k, pl.ds(shifts[k], WIN), :]


def cut_windows(latents, labels, slot_source, episode_pick, window_start, position):
    smem = pl.BlockSpec(memory_space=pltpu.SMEM)
    vmem = pl.BlockSpec(memory_space=pltpu.VMEM)
    hbm = pl.BlockSpec(memory_space=pltpu.HBM)
    return pl.pallas_call(
        cut_kernel,
        out_shape=(
            jax.ShapeDtypeStruct((8, 512, 128), BF),
            jax.ShapeDtypeStruct((512, 128), BF),
            jax.ShapeDtypeStruct((512, 128), F32),
        ),
        in_specs=[smem, vmem, vmem, vmem, hbm, hbm],
        out_specs=(vmem, vmem, vmem),
        scratch_shapes=[
            pltpu.VMEM((2, WIN + 16, 128), BF),
            pltpu.VMEM((2, WIN + 16, 128), BF),
            pltpu.VMEM((2, WIN + 16, 128), F32),
            pltpu.SemaphoreType.DMA((2, 2)),
        ],
        compiler_params=pltpu.CompilerParams(vmem_limit_bytes=60 * 2**20),
        name="cut_windows",
    )(
        position.reshape(1),
        slot_source.reshape(1, 128),
        episode_pick.reshape(1, 128),
        window_start.reshape(1, 128),
        latents,
        labels,
    )


def three_parts(x):
    high = lax.reduce_precision(x, 8, 7)
    rest = x - high
    mid = lax.reduce_precision(rest, 8, 7)
    return jnp.concatenate([high, mid, rest - mid]).astype(BF)


def on_device(
    latents, labels, slot_source, episode_pick, window_start, proj_weight, norm_gain, head_weight
):
    position = lax.axis_index("dp")
    c, xl, zl, zh = position % 2, (position // 2) % 2, (position // 4) % 4, position // 16
    own_copies, own, targets = cut_windows(
        latents, labels, slot_source, episode_pick, window_start, position
    )

    pieces = exchange(
        jnp.transpose(own.reshape(2, 64, 4, 128), (1, 0, 2, 3)).reshape(128, 4, 128), "dp"
    )
    proj = gather(proj_weight, "dp", Z_GROUPS).reshape(16, 16, 768)
    proj, pieces = tie(proj, pieces)
    own_copies, pieces = tie(own_copies, pieces)

    gathered = exchange(own_copies, "mp")
    proj = pair(proj, permute(proj, to_xlo), xl)
    proj = pair(proj, permute(proj, to_core), c)
    proj = jnp.transpose(proj, (2, 1, 0, 3, 4)).reshape(1024, 768)
    ordered, gathered = tie(pieces[slot_source], gathered)
    arrived = exchange(ordered, "dp")
    inputs = jnp.transpose(gathered, (1, 0, 2)).reshape(512, 1024)

    hidden = jnp.dot(inputs, proj, preferred_element_type=F32)
    local_mean = jnp.sum(hidden, axis=1) / 768
    centred = hidden - local_mean[:, None]
    square = jnp.sum(centred * centred, axis=1)
    scaled = (centred * norm_gain).astype(BF)
    partial = jnp.dot(scaled, head_weight, preferred_element_type=F32).astype(BF)
    gain_head = jnp.sum(norm_gain[:, None] * head_weight.astype(F32), axis=0)
    sums = jnp.concatenate(
        [local_mean.reshape(4, 128), square.reshape(4, 128), gain_head[None]], axis=0
    )
    sent = jnp.concatenate([partial, three_parts(sums), jnp.zeros((101, 128), BF)], axis=0)
    sent, arrived = tie(copies(sent, 8), arrived)
    all_sent = exchange(sent, "mp")
    arrived = jnp.transpose(arrived.reshape(64, 2, 4, 128), (1, 0, 2, 3)).reshape(512, 128)
    arrived, all_sent = tie(copies(arrived, 8), all_sent)
    there = exchange(arrived, "mp")
    summed = jnp.sum(all_sent[:, :512].astype(F32), axis=0)
    sums = jnp.sum(all_sent[:, 512:539].astype(F32).reshape(8, 3, 9, 128), axis=1)
    means = sums[:, :4].reshape(8, 512)
    squares = sums[:, 4:8].reshape(8, 512)
    gain_heads = sums[:, 8]

    def statistics(means, squares):
        mean = jnp.sum(means, axis=0) / 8
        off = means - mean
        variance = (jnp.sum(squares, axis=0) + 768 * jnp.sum(off * off, axis=0)) / D
        return mean, off, lax.rsqrt(variance + EPSILON)

    row_mean, off, row_scale = statistics(means, squares)
    shift = sum(off[m][:, None] * gain_heads[m][None, :] for m in range(8))
    predicted = row_scale[:, None] * (summed + shift)
    error_grad = ((predicted - targets) / math.sqrt(32768)).astype(BF)
    error_wide = error_grad.astype(F32)
    normed = (hidden - row_mean[:, None]) * row_scale[:, None]
    features_here = (normed * norm_gain).astype(BF)
    head_term = lax.dot_general(
        error_grad, features_here, (((0,), (0,)), ((), ())), preferred_element_type=F32
    )
    back_feat = lax.dot_general(
        error_grad, head_weight, (((1,), (1,)), ((), ())), preferred_element_type=F32
    )
    gain_term = jnp.sum(back_feat * normed, axis=0)
    first_sum = jnp.sum(error_wide * jnp.sum(gain_heads, axis=0), axis=1)
    second_sum = jnp.sum(error_wide * predicted, axis=1)
    back_hidden = (
        row_scale[:, None]
        * (
            back_feat * norm_gain
            - first_sum[:, None] / D
            - normed * (second_sum[:, None] / D)
        )
    ).astype(BF)
    full_term = lax.dot_general(
        inputs, back_hidden, (((0,), (0,)), ((), ())), preferred_element_type=F32
    )

    gain_rows = jnp.pad(gain_term.reshape(16, 1, 48), ((0, 0), (0, 7), (0, 80)))
    head_rows = jnp.concatenate([head_term.reshape(16, 8, 768), gain_rows], axis=2).astype(BF)
    head_rows, there = tie(head_rows, there)
    part = exchange(head_rows, "dp", Z_GROUPS)
    blocks = full_term.reshape(16, 2, 2, 16, 768)
    kept = take(blocks, c, 2) + permute(take(blocks, 1 - c, 2), to_core)
    part, kept = tie(part, kept)

    inputs_there = jnp.transpose(there, (1, 0, 2)).reshape(512, 1024)
    hidden_there = jnp.dot(inputs_there, proj, preferred_element_type=F32)
    local_mean = jnp.sum(hidden_there, axis=1) / 768
    centred = hidden_there - local_mean[:, None]
    square = jnp.sum(centred * centred, axis=1)
    sums = jnp.concatenate([local_mean.reshape(4, 128), square.reshape(4, 128)], axis=0)
    sums, part = tie(copies(sums, 8), part)
    sums = exchange(sums, "mp")

    part = jnp.sum(part.astype(F32), axis=0)
    part = part + permute(part, to_core)
    kept = take(kept, xl, 1) + permute(take(kept, 1 - xl, 1).astype(BF), to_xlo).astype(F32)
    part, kept = tie(part, kept)
    part = part + permute(part, to_xlo)
    kept = scatter4(jnp.transpose(kept.reshape(4, 4, 16, 768), (1, 0, 2, 3)), zl, to_zl)
    part, kept = tie(part, kept)
    part, sums = tie(copies(part.astype(BF), 16), sums)
    whole = exchange(part, "dp", Z_GROUPS).astype(F32)
    grad_head = jnp.transpose(whole[:, :, :768].reshape(128, 768))
    grad_gain = whole[:, 0, 768:816].reshape(768)
    grad_proj = scatter4(kept, zh, to_zh)

    mean, _, scale = statistics(sums[:, :4].reshape(8, 512), sums[:, 4:].reshape(8, 512))
    features = (((hidden_there - mean[:, None]) * scale[:, None]) * norm_gain).astype(BF)
    return (grad_proj, grad_head, grad_gain, features)


def solution(mesh):
    in_specs = (
        P("dp", None, "mp"),
        P("dp", None, None),
        P(),
        P(),
        P(),
        P("dp", "mp"),
        P("mp"),
        P("mp", None),
    )
    out_specs = (P("dp", "mp"), P("mp", None), P("mp"), P("dp", "mp"))
    return jax.shard_map(
        on_device, mesh=mesh, in_specs=in_specs, out_specs=out_specs, check_vma=False
    )
```

```python
import math

import jax
import jax.numpy as jnp
from jax import lax
from jax.experimental import pallas as pl
from jax.experimental.pallas import tpu as pltpu
from jax.sharding import PartitionSpec as P

D = 6144
WIN = 256
EPSILON = 1e-05
BF = jnp.bfloat16
F32 = jnp.float32

N_DP = 64
Z_GROUPS = [[z * 4 + q for z in range(16)] for q in range(4)]
ZH_GROUPS = [[zh * 16 + q for zh in range(4)] for q in range(16)]
ZL_GROUPS = [[zh * 16 + zl * 4 + q for zl in range(4)] for zh in range(4) for q in range(4)]


def to_core(i):
    return i ^ 1


def to_xlo(i):
    return i ^ 2


def to_zl(k):
    return lambda i: (i & ~12) | ((i + 4 * k) & 12)


def to_zh(k):
    return lambda i: (i + 16 * k) % N_DP


def permute(x, target):
    return lax.ppermute(x, "dp", [(i, target(i)) for i in range(N_DP)])


def exchange(x, axis, groups=None):
    return lax.all_to_all(
        x, axis, split_axis=0, concat_axis=0, tiled=True, axis_index_groups=groups
    )


def gather(x, axis, groups=None):
    return lax.all_gather(x, axis, axis=0, tiled=True, axis_index_groups=groups)


def copies(x, n):
    return jnp.broadcast_to(x[None], (n,) + x.shape)


def take(x, index, axis):
    return lax.dynamic_index_in_dim(x, index, axis, keepdims=False)


def pair(mine, other, index):
    return jnp.where(index == 0, jnp.stack([mine, other]), jnp.stack([other, mine]))


def scatter4(blocks, index, to):
    total = take(blocks, index, 0)
    for k in (1, 2, 3):
        sent = take(blocks, (index + k) % 4, 0).astype(BF)
        total = total + permute(sent, to(k)).astype(F32)
    return total


def tie(x, y):
    return lax.optimization_barrier((x, y))


PEERS = 64


def cut_kernel(
    position_ref, slot_ref, pick_ref, start_ref, latents_ref, labels_ref,
    pieces_ref, lat_held, lab_held, wide, sems,
):
    shifts, moves = [], []
    for k in range(2):
        here = slot_ref[...] == position_ref[0] * 2 + k
        episode = jnp.sum(jnp.where(here, pick_ref[...], 0).astype(F32)).astype(jnp.int32)
        start = jnp.sum(jnp.where(here, start_ref[...], 0).astype(F32)).astype(jnp.int32)
        first = pl.multiple_of(jnp.minimum(start // 16, 15) * 16, 16)
        shifts.append(start - first)
        for n, (store, held) in enumerate(((latents_ref, lat_held), (labels_ref, lab_held))):
            move = pltpu.make_async_copy(
                store.at[episode, pl.ds(first, WIN + 16), :], held.at[k], sems.at[n, k]
            )
            move.start()
            moves.append(move)
    part = position_ref[1]
    for k in range(2):
        moves[2 * k].wait()
        moves[2 * k + 1].wait()
        wide[0, : WIN + 16] = lat_held[k].astype(F32)
        wide[1, : WIN + 16] = lab_held[k].astype(F32)
        for r in range(4):
            rows = wide[0, pl.ds(shifts[k] + r, PEERS, stride=4), :]
            pieces_ref[k, :, r * 128 : (r + 1) * 128] = rows.astype(BF)
        rows = wide[1, pl.ds(shifts[k] + part // 2, PEERS, stride=4), :]
        rows = jnp.where(part % 2 == 0, rows, pltpu.roll(rows, 64, 1))
        pieces_ref[k, :, 512:640] = rows.astype(BF)


def cut_windows(latents, labels, slot_source, episode_pick, window_start, position, part):
    smem = pl.BlockSpec(memory_space=pltpu.SMEM)
    vmem = pl.BlockSpec(memory_space=pltpu.VMEM)
    hbm = pl.BlockSpec(memory_space=pltpu.HBM)
    return pl.pallas_call(
        cut_kernel,
        out_shape=jax.ShapeDtypeStruct((2, PEERS, 640), BF),
        in_specs=[smem, vmem, vmem, vmem, hbm, hbm],
        out_specs=vmem,
        scratch_shapes=[
            pltpu.VMEM((2, WIN + 16, 128), BF),
            pltpu.VMEM((2, WIN + 16, 128), BF),
            pltpu.VMEM((2, WIN + 24, 128), F32),
            pltpu.SemaphoreType.DMA((2, 2)),
        ],
        compiler_params=pltpu.CompilerParams(vmem_limit_bytes=60 * 2**20),
        name="cut_windows",
    )(
        jnp.stack([position, part]),
        slot_source.reshape(1, 128),
        episode_pick.reshape(1, 128),
        window_start.reshape(1, 128),
        latents,
        labels,
    )


def order_kernel(arrived_ref, copies_ref, wide):
    for w in range(2):
        for r in range(4):
            wide[pl.ds(w * WIN + r, PEERS, stride=4), :] = arrived_ref[
                w, :, r * 128 : (r + 1) * 128
            ].astype(F32)
    first = arrived_ref[0, :, 512:640].astype(F32)
    second = pltpu.roll(arrived_ref[1, :, 512:640].astype(F32), 64, 1)
    lane = lax.broadcasted_iota(jnp.int32, (PEERS, 128), 1)
    both = jnp.where(lane < 64, first, second).astype(BF)
    rows = wide[...].astype(BF)
    for m in range(8):
        copies_ref[m, :512, :] = rows
        copies_ref[m, 512:576, :] = both
        copies_ref[m, 576:640, :] = jnp.zeros((64, 128), BF)


def order_rows(arrived):
    vmem = pl.BlockSpec(memory_space=pltpu.VMEM)
    return pl.pallas_call(
        order_kernel,
        out_shape=jax.ShapeDtypeStruct((8, 640, 128), BF),
        in_specs=[vmem],
        out_specs=vmem,
        scratch_shapes=[pltpu.VMEM((512, 128), F32)],
        compiler_params=pltpu.CompilerParams(vmem_limit_bytes=60 * 2**20),
        name="order_rows",
    )(arrived)


CHUNK = 128
ROWS = 512
SENT = 640


def two_parts(x):
    high = x.astype(BF).astype(F32)
    return high, x - high


def forward_kernel(
    place_ref, gathered_ref, own_ref, core_ref, gain_ref, head_ref,
    sent_ref, hidden_ref, inputs_ref, proj, scaled,
):
    xl, c = place_ref[0], place_ref[1]
    for zl in range(4):
        for zh in range(4):
            for dx in range(2):
                for dc, ref in enumerate((own_ref, core_ref)):
                    block = (zh * 4 + zl) * 4 + (xl ^ dx) * 2 + (c ^ dc)
                    proj[pl.ds(pl.multiple_of(block * 16, 16), 16), :] = ref[zl, dx, zh]
    for m in range(8):
        inputs_ref[:, m * 128 : (m + 1) * 128] = gathered_ref[m, :ROWS, :]
    gain = gain_ref[...]
    lane = lax.broadcasted_iota(jnp.int32, (CHUNK, 128), 1)
    row = lax.broadcasted_iota(jnp.int32, (16, 768), 0)
    gain_high, rest = two_parts(gain)
    gain_mid, gain_low = two_parts(rest)
    gains = jnp.where(
        row == 0, gain_high, jnp.where(row == 1, gain_mid, jnp.where(row == 2, gain_low, 0.0))
    )
    gain_head = jnp.sum(
        jnp.dot(gains.astype(BF), head_ref[...], preferred_element_type=F32), axis=0, keepdims=True
    )
    high, rest = two_parts(gain_head)
    mid, low = two_parts(rest)
    row = lax.broadcasted_iota(jnp.int32, (16, 128), 0)
    gain_head = jnp.where(row == 0, high, jnp.where(row == 1, mid, jnp.where(row == 2, low, 0.0)))
    for m in range(8):
        sent_ref[m, 576:592, :] = gain_head.astype(BF)
        sent_ref[m, 592:640, :] = jnp.zeros((48, 128), BF)

    for n in range(0, 768, 256):
        hidden_ref[:, n : n + 256] = jnp.dot(
            inputs_ref[...], proj[:, n : n + 256], preferred_element_type=F32
        )
    for i in range(0, ROWS, CHUNK):
        hidden = hidden_ref[i : i + CHUNK, :]
        mean = jnp.sum(hidden, axis=1, keepdims=True) / 768
        centred = hidden - mean
        square = jnp.sum(centred * centred, axis=1, keepdims=True)
        scaled[i : i + CHUNK, :] = (centred * gain).astype(BF)
        parts = []
        for value in (mean, square):
            high, rest = two_parts(value)
            mid, low = two_parts(rest)
            parts += [high, mid, low]
        packed = jnp.zeros((CHUNK, 128), F32)
        for k, value in enumerate(parts):
            packed = jnp.where(lane == k, value, packed)
        packed = packed.T[:16].astype(BF)
        start = ROWS + i // 8
        for m in range(8):
            sent_ref[m, start : start + 16, :] = packed
    partial = jnp.dot(scaled[...], head_ref[...], preferred_element_type=F32).astype(BF)
    for m in range(8):
        sent_ref[m, :ROWS, :] = partial


def backward_kernel(
    sent_ref, labels_ref, hidden_ref, gain_ref, head_ref,
    features_ref, back_ref, head_rows_ref, targets, errors, gain_sum,
):
    gain = gain_ref[...]
    lane = lax.broadcasted_iota(jnp.int32, (64, 128), 1)
    for r in range(4):
        one = labels_ref[2 * r].astype(F32)
        two = labels_ref[2 * r + 1].astype(F32)
        targets[pl.ds(r, 64, stride=4), :] = jnp.where(lane < 64, one, pltpu.roll(two, 64, 1))
        targets[pl.ds(WIN + r, 64, stride=4), :] = jnp.where(
            lane < 64, pltpu.roll(one, 64, 1), two
        )
    gain_heads = [
        jnp.sum(sent_ref[m, 576:592, :].astype(F32), axis=0, keepdims=True) for m in range(8)
    ]
    gain_head = sum(gain_heads)
    gain_sum[...] = jnp.zeros((8, 768), F32)
    lane = lax.broadcasted_iota(jnp.int32, (CHUNK, 128), 1) % 16

    for i in range(ROWS // CHUNK):
        rows = slice(i * CHUNK, (i + 1) * CHUNK)
        start = ROWS + i * 16
        stats = jnp.concatenate(
            [sent_ref[m, start : start + 16, :].astype(F32) for m in range(8)], axis=0
        ).T
        summed = sent_ref[0, rows, :].astype(F32)
        for m in range(1, 8):
            summed += sent_ref[m, rows, :].astype(F32)
        means = [
            jnp.sum(stats[:, 16 * m : 16 * m + 3], axis=1, keepdims=True) for m in range(8)
        ]
        mean = sum(means) / 8
        squares = jnp.sum(
            jnp.where((lane >= 3) & (lane < 6), stats, 0.0), axis=1, keepdims=True
        )
        for m in range(8):
            off = means[m] - mean
            squares += 768 * (off * off)
            summed += off * gain_heads[m]
        scale = lax.rsqrt(squares / D + EPSILON)
        predicted = scale * summed
        error = ((predicted - targets[rows, :]) / math.sqrt(32768)).astype(BF)
        errors[rows, :] = error
        wide = error.astype(F32)
        first = jnp.sum(wide * gain_head, axis=1, keepdims=True) / D
        second = jnp.sum(wide * predicted, axis=1, keepdims=True) / D
        normed = (hidden_ref[rows, :] - mean) * scale
        features_ref[rows, :] = (normed * gain).astype(BF)
        back = lax.dot_general(
            error, head_ref[...], (((1,), (1,)), ((), ())), preferred_element_type=F32
        )
        gain_sum[...] += jnp.sum((back * normed).reshape(CHUNK // 8, 8, 768), axis=0)
        back_ref[rows, :] = (scale * (back * gain - first - normed * second)).astype(BF)

    head_rows_ref[:, :768] = lax.dot_general(
        errors[...], features_ref[...], (((0,), (0,)), ((), ())), preferred_element_type=F32
    ).astype(BF)
    total = jnp.broadcast_to(jnp.sum(gain_sum[...], axis=0, keepdims=True), (8, 768))
    place = lax.broadcasted_iota(jnp.int32, (8, 128), 0)
    lane = lax.broadcasted_iota(jnp.int32, (8, 128), 1)
    for z in range(0, 16, 2):
        pair_rows = []
        for y in (z, z + 1):
            turned = total if y == 0 else pltpu.roll(total, 768 - 48 * y, 1)
            pair_rows.append(jnp.where((place == 0) & (lane < 48), turned[:, :128], 0.0))
        head_rows_ref[z * 8 : z * 8 + 16, 768:] = jnp.concatenate(pair_rows, axis=0).astype(BF)


def weight_kernel(place_ref, turned_ref, back_ref, kept_ref, given_ref, held):
    xl, c = place_ref[0], place_ref[1]
    for dc, out_ref in enumerate((kept_ref, given_ref)):
        for dx in range(2):
            for zl in range(4):
                for zh in range(4):
                    block = ((zh * 4 + zl) * 2 + (xl ^ dx)) * 2 + (c ^ dc)
                    row = dx * 256 + (zl * 4 + zh) * 16
                    held[dc, row : row + 16, :] = turned_ref[
                        pl.ds(pl.multiple_of(block * 16, 16), 16), :
                    ]
        for n in range(0, 768, 256):
            out_ref[:, n : n + 256] = jnp.dot(
                held[dc], back_ref[:, n : n + 256], preferred_element_type=F32
            ).astype(out_ref.dtype)


VMEM_SPEC = pl.BlockSpec(memory_space=pltpu.VMEM)
SMEM_SPEC = pl.BlockSpec(memory_space=pltpu.SMEM)


def call(kernel, name, outs, scratch, specs, *args):
    return pl.pallas_call(
        kernel,
        out_shape=outs,
        in_specs=specs,
        out_specs=jax.tree.map(lambda _: VMEM_SPEC, outs),
        scratch_shapes=scratch,
        compiler_params=pltpu.CompilerParams(vmem_limit_bytes=60 * 2**20),
        name=name,
    )(*args)


def array(shape, dtype):
    return jax.ShapeDtypeStruct(shape, dtype)


def on_device(
    latents, labels, slot_source, episode_pick, window_start, proj_weight, norm_gain, head_weight
):
    position = lax.axis_index("dp")
    c, xl, zl, zh = position % 2, (position // 2) % 2, (position // 4) % 4, position // 16
    pieces = cut_windows(
        latents, labels, slot_source, episode_pick, window_start, position, lax.axis_index("mp")
    )
    pieces = exchange(jnp.transpose(pieces, (1, 0, 2)), "dp")
    proj_own = gather(proj_weight, "dp", ZH_GROUPS)
    pieces, proj_own = tie(pieces, proj_own)
    proj_xlo = permute(proj_own, to_xlo)
    ordered = pieces.reshape(128, 640)[slot_source].reshape(PEERS, 2, 640)
    ordered, proj_own = tie(ordered, proj_own)
    arrived = exchange(ordered, "dp")
    proj_own = gather(jnp.concatenate([proj_own, proj_xlo]), "dp", ZL_GROUPS)
    proj_own = proj_own.reshape(4, 2, 4, 16, 768)
    arrived, proj_own = tie(arrived, proj_own)
    proj_core = permute(proj_own, to_core)
    gathered = exchange(order_rows(jnp.transpose(arrived, (1, 0, 2))), "mp")

    place = jnp.stack([xl, c])
    gain = norm_gain.reshape(1, 768)
    sent, hidden, inputs = call(
        forward_kernel,
        "forward",
        (array((8, SENT, 128), BF), array((ROWS, 768), F32), array((ROWS, 1024), BF)),
        [pltpu.VMEM((1024, 768), BF), pltpu.VMEM((ROWS, 768), BF)],
        [SMEM_SPEC] + [VMEM_SPEC] * 5,
        place, gathered, proj_own, proj_core, gain, head_weight,
    )
    all_sent = exchange(sent, "mp")
    features, back_hidden, head_rows = call(
        backward_kernel,
        "backward",
        (array((ROWS, 768), BF), array((ROWS, 768), BF), array((128, 896), BF)),
        [pltpu.VMEM((ROWS, 128), F32), pltpu.VMEM((ROWS, 128), BF), pltpu.VMEM((8, 768), F32)],
        [VMEM_SPEC] * 5,
        all_sent, gathered[:, 512:576], hidden, gain, head_weight,
    )
    kept, given = call(
        weight_kernel,
        "weight",
        (array((ROWS, 768), F32), array((ROWS, 768), BF)),
        [pltpu.VMEM((2, ROWS, ROWS), BF)],
        [SMEM_SPEC] + [VMEM_SPEC] * 2,
        place, jnp.transpose(inputs), back_hidden,
    )

    kept = kept + permute(given, to_core).astype(F32)
    head_rows, kept = tie(head_rows, kept)
    part = exchange(head_rows.reshape(16, 8, 896), "dp", Z_GROUPS)
    kept = kept[:256] + permute(kept[256:].astype(BF), to_xlo).astype(F32)
    kept = scatter4(kept.reshape(4, 64, 768), zl, to_zl)
    part, kept = tie(part, kept)
    part = jnp.sum(part.astype(F32), axis=0)
    part = part + permute(part, to_core)
    part = part + permute(part, to_xlo)
    grad_proj = exchange(kept.astype(BF).reshape(4, 16, 768), "dp", ZH_GROUPS)
    part, grad_proj = tie(part, grad_proj)
    grad_proj = jnp.sum(grad_proj.astype(F32), axis=0)
    whole = exchange(copies(part.astype(BF), 16), "dp", Z_GROUPS).astype(F32)
    grad_head = jnp.transpose(whole[:, :, :768].reshape(128, 768))
    grad_gain = whole[:, 0, 768:816].reshape(768)
    return (grad_proj, grad_head, grad_gain, features)


def solution(mesh):
    in_specs = (
        P("dp", None, "mp"),
        P("dp", None, None),
        P(),
        P(),
        P(),
        P("dp", "mp"),
        P("mp"),
        P("mp", None),
    )
    out_specs = (P("dp", "mp"), P("mp", None), P("mp"), P("dp", "mp"))
    return jax.shard_map(
        on_device, mesh=mesh, in_specs=in_specs, out_specs=out_specs, check_vma=False
    )
```

```python
import math

import jax
import jax.numpy as jnp
from jax import lax
from jax.experimental import pallas as pl
from jax.experimental.pallas import tpu as pltpu
from jax.sharding import PartitionSpec as P

D = 6144
WIN = 256
EPSILON = 1e-05
BF = jnp.bfloat16
F32 = jnp.float32

N_DP = 64
Z_GROUPS = [[z * 4 + q for z in range(16)] for q in range(4)]
ZH_GROUPS = [[zh * 16 + q for zh in range(4)] for q in range(16)]
ZL_GROUPS = [[zh * 16 + zl * 4 + q for zl in range(4)] for zh in range(4) for q in range(4)]


def to_core(i):
    return i ^ 1


def to_xlo(i):
    return i ^ 2


def to_zl(k):
    return lambda i: (i & ~12) | ((i + 4 * k) & 12)


def to_zh(k):
    return lambda i: (i + 16 * k) % N_DP


def permute(x, target):
    return lax.ppermute(x, "dp", [(i, target(i)) for i in range(N_DP)])


def exchange(x, axis, groups=None):
    return lax.all_to_all(
        x, axis, split_axis=0, concat_axis=0, tiled=True, axis_index_groups=groups
    )


def gather(x, axis, groups=None):
    return lax.all_gather(x, axis, axis=0, tiled=True, axis_index_groups=groups)


def copies(x, n):
    return jnp.broadcast_to(x[None], (n,) + x.shape)


def take(x, index, axis):
    return lax.dynamic_index_in_dim(x, index, axis, keepdims=False)


def pair(mine, other, index):
    return jnp.where(index == 0, jnp.stack([mine, other]), jnp.stack([other, mine]))


def tie(x, y):
    return lax.optimization_barrier((x, y))


PEERS = 64


def cut_kernel(
    position_ref, slot_ref, pick_ref, start_ref, latents_ref, labels_ref,
    pieces_ref, lat_held, lab_held, wide, sems,
):
    shifts, moves = [], []
    for k in range(2):
        here = slot_ref[...] == position_ref[0] * 2 + k
        episode = jnp.sum(jnp.where(here, pick_ref[...], 0).astype(F32)).astype(jnp.int32)
        start = jnp.sum(jnp.where(here, start_ref[...], 0).astype(F32)).astype(jnp.int32)
        first = pl.multiple_of(jnp.minimum(start // 16, 15) * 16, 16)
        shifts.append(start - first)
        for n, (store, held) in enumerate(((latents_ref, lat_held), (labels_ref, lab_held))):
            move = pltpu.make_async_copy(
                store.at[episode, pl.ds(first, WIN + 16), :], held.at[k], sems.at[n, k]
            )
            move.start()
            moves.append(move)
    part = position_ref[1]
    for k in range(2):
        moves[2 * k].wait()
        moves[2 * k + 1].wait()
        wide[0, : WIN + 16] = lat_held[k].astype(F32)
        wide[1, : WIN + 16] = lab_held[k].astype(F32)
        for r in range(4):
            rows = wide[0, pl.ds(shifts[k] + r, PEERS, stride=4), :]
            pieces_ref[k, :, r * 128 : (r + 1) * 128] = rows.astype(BF)
        rows = wide[1, pl.ds(shifts[k] + part // 2, PEERS, stride=4), :]
        rows = jnp.where(part % 2 == 0, rows, pltpu.roll(rows, 64, 1))
        pieces_ref[k, :, 512:640] = rows.astype(BF)


def cut_windows(latents, labels, slot_source, episode_pick, window_start, position, part):
    smem = pl.BlockSpec(memory_space=pltpu.SMEM)
    vmem = pl.BlockSpec(memory_space=pltpu.VMEM)
    hbm = pl.BlockSpec(memory_space=pltpu.HBM)
    return pl.pallas_call(
        cut_kernel,
        out_shape=jax.ShapeDtypeStruct((2, PEERS, 640), BF),
        in_specs=[smem, vmem, vmem, vmem, hbm, hbm],
        out_specs=vmem,
        scratch_shapes=[
            pltpu.VMEM((2, WIN + 16, 128), BF),
            pltpu.VMEM((2, WIN + 16, 128), BF),
            pltpu.VMEM((2, WIN + 24, 128), F32),
            pltpu.SemaphoreType.DMA((2, 2)),
        ],
        compiler_params=pltpu.CompilerParams(vmem_limit_bytes=60 * 2**20),
        name="cut_windows",
    )(
        jnp.stack([position, part]),
        slot_source.reshape(1, 128),
        episode_pick.reshape(1, 128),
        window_start.reshape(1, 128),
        latents,
        labels,
    )


def order_kernel(arrived_ref, copies_ref, wide):
    for w in range(2):
        for r in range(4):
            wide[pl.ds(w * WIN + r, PEERS, stride=4), :] = arrived_ref[
                w, :, r * 128 : (r + 1) * 128
            ].astype(F32)
    first = arrived_ref[0, :, 512:640].astype(F32)
    second = pltpu.roll(arrived_ref[1, :, 512:640].astype(F32), 64, 1)
    lane = lax.broadcasted_iota(jnp.int32, (PEERS, 128), 1)
    both = jnp.where(lane < 64, first, second).astype(BF)
    rows = wide[...].astype(BF)
    for m in range(8):
        copies_ref[m, :512, :] = rows
        copies_ref[m, 512:576, :] = both
        copies_ref[m, 576:640, :] = jnp.zeros((64, 128), BF)


def order_rows(arrived):
    vmem = pl.BlockSpec(memory_space=pltpu.VMEM)
    return pl.pallas_call(
        order_kernel,
        out_shape=jax.ShapeDtypeStruct((8, 640, 128), BF),
        in_specs=[vmem],
        out_specs=vmem,
        scratch_shapes=[pltpu.VMEM((512, 128), F32)],
        compiler_params=pltpu.CompilerParams(vmem_limit_bytes=60 * 2**20),
        name="order_rows",
    )(arrived)


CHUNK = 128
ROWS = 512
SENT = 640


def two_parts(x):
    high = x.astype(BF).astype(F32)
    return high, x - high


def forward_kernel(
    place_ref, gathered_ref, own_ref, core_ref, gain_ref, head_ref,
    sent_ref, hidden_ref, inputs_ref, proj, scaled,
):
    xl, c = place_ref[0], place_ref[1]
    for zl in range(4):
        for zh in range(4):
            for dx in range(2):
                for dc, ref in enumerate((own_ref, core_ref)):
                    block = (zh * 4 + zl) * 4 + (xl ^ dx) * 2 + (c ^ dc)
                    proj[pl.ds(pl.multiple_of(block * 16, 16), 16), :] = ref[zl, dx, zh]
    for m in range(8):
        inputs_ref[:, m * 128 : (m + 1) * 128] = gathered_ref[m, :ROWS, :]
    gain = gain_ref[...]
    lane = lax.broadcasted_iota(jnp.int32, (CHUNK, 128), 1)
    row = lax.broadcasted_iota(jnp.int32, (16, 768), 0)
    gain_high, rest = two_parts(gain)
    gain_mid, gain_low = two_parts(rest)
    gains = jnp.where(
        row == 0, gain_high, jnp.where(row == 1, gain_mid, jnp.where(row == 2, gain_low, 0.0))
    )
    gain_head = jnp.sum(
        jnp.dot(gains.astype(BF), head_ref[...], preferred_element_type=F32), axis=0, keepdims=True
    )
    high, rest = two_parts(gain_head)
    mid, low = two_parts(rest)
    row = lax.broadcasted_iota(jnp.int32, (16, 128), 0)
    gain_head = jnp.where(row == 0, high, jnp.where(row == 1, mid, jnp.where(row == 2, low, 0.0)))
    for m in range(8):
        sent_ref[m, 576:592, :] = gain_head.astype(BF)
        sent_ref[m, 592:640, :] = jnp.zeros((48, 128), BF)

    for n in range(0, 768, 256):
        hidden_ref[:, n : n + 256] = jnp.dot(
            inputs_ref[...], proj[:, n : n + 256], preferred_element_type=F32
        )
    for i in range(0, ROWS, CHUNK):
        hidden = hidden_ref[i : i + CHUNK, :]
        mean = jnp.sum(hidden, axis=1, keepdims=True) / 768
        centred = hidden - mean
        square = jnp.sum(centred * centred, axis=1, keepdims=True)
        scaled[i : i + CHUNK, :] = (centred * gain).astype(BF)
        parts = []
        for value in (mean, square):
            high, rest = two_parts(value)
            mid, low = two_parts(rest)
            parts += [high, mid, low]
        packed = jnp.zeros((CHUNK, 128), F32)
        for k, value in enumerate(parts):
            packed = jnp.where(lane == k, value, packed)
        packed = packed.T[:16].astype(BF)
        start = ROWS + i // 8
        for m in range(8):
            sent_ref[m, start : start + 16, :] = packed
    partial = jnp.dot(scaled[...], head_ref[...], preferred_element_type=F32).astype(BF)
    for m in range(8):
        sent_ref[m, :ROWS, :] = partial


def backward_kernel(
    sent_ref, labels_ref, hidden_ref, gain_ref, head_ref,
    features_ref, back_ref, head_rows_ref, targets, errors, gain_sum,
):
    gain = gain_ref[...]
    lane = lax.broadcasted_iota(jnp.int32, (64, 128), 1)
    for r in range(4):
        one = labels_ref[2 * r].astype(F32)
        two = labels_ref[2 * r + 1].astype(F32)
        targets[pl.ds(r, 64, stride=4), :] = jnp.where(lane < 64, one, pltpu.roll(two, 64, 1))
        targets[pl.ds(WIN + r, 64, stride=4), :] = jnp.where(
            lane < 64, pltpu.roll(one, 64, 1), two
        )
    gain_heads = [
        jnp.sum(sent_ref[m, 576:592, :].astype(F32), axis=0, keepdims=True) for m in range(8)
    ]
    gain_head = sum(gain_heads)
    gain_sum[...] = jnp.zeros((8, 768), F32)

    for i in range(ROWS // CHUNK):
        rows = slice(i * CHUNK, (i + 1) * CHUNK)
        start = ROWS + i * 16
        stats = [sent_ref[m, start : start + 16, :].astype(F32) for m in range(8)]
        means = [part[0:1] + part[1:2] + part[2:3] for part in stats]
        mean = sum(means) / 8
        offs = [value - mean for value in means]
        squares = sum(part[3:4] + part[4:5] + part[5:6] for part in stats)
        squares += 768 * sum(off * off for off in offs)
        scale = lax.rsqrt(squares / D + EPSILON)
        turned = jnp.concatenate(offs + [mean, scale, jnp.zeros((118, 128), F32)], axis=0).T
        mean, scale = turned[:, 8:9], turned[:, 9:10]
        summed = sent_ref[0, rows, :].astype(F32)
        for m in range(1, 8):
            summed += sent_ref[m, rows, :].astype(F32)
        for m in range(8):
            summed += turned[:, m : m + 1] * gain_heads[m]
        predicted = scale * summed
        error = ((predicted - targets[rows, :]) / math.sqrt(32768)).astype(BF)
        errors[rows, :] = error
        wide = error.astype(F32)
        first = jnp.sum(wide * gain_head, axis=1, keepdims=True) / D
        second = jnp.sum(wide * predicted, axis=1, keepdims=True) / D
        normed = (hidden_ref[rows, :] - mean) * scale
        features_ref[rows, :] = (normed * gain).astype(BF)
        back = lax.dot_general(
            error, head_ref[...], (((1,), (1,)), ((), ())), preferred_element_type=F32
        )
        gain_sum[...] += jnp.sum((back * normed).reshape(CHUNK // 8, 8, 768), axis=0)
        back_ref[rows, :] = (scale * (back * gain - first - normed * second)).astype(BF)

    head_rows_ref[:, :768] = lax.dot_general(
        errors[...], features_ref[...], (((0,), (0,)), ((), ())), preferred_element_type=F32
    ).astype(BF)
    total = jnp.broadcast_to(jnp.sum(gain_sum[...], axis=0, keepdims=True), (8, 768))
    place = lax.broadcasted_iota(jnp.int32, (8, 128), 0)
    lane = lax.broadcasted_iota(jnp.int32, (8, 128), 1)
    for z in range(0, 16, 2):
        pair_rows = []
        for y in (z, z + 1):
            turned = total if y == 0 else pltpu.roll(total, 768 - 48 * y, 1)
            pair_rows.append(jnp.where((place == 0) & (lane < 48), turned[:, :128], 0.0))
        head_rows_ref[z * 8 : z * 8 + 16, 768:] = jnp.concatenate(pair_rows, axis=0).astype(BF)


def weight_kernel(place_ref, turned_ref, back_ref, kept_ref, given_ref, held):
    xl, c = place_ref[0], place_ref[1]
    for dc, out_ref in enumerate((kept_ref, given_ref)):
        for dx in range(2):
            for zl in range(4):
                for zh in range(4):
                    block = ((zh * 4 + zl) * 2 + (xl ^ dx)) * 2 + (c ^ dc)
                    row = dx * 256 + (zl * 4 + zh) * 16
                    held[dc, row : row + 16, :] = turned_ref[
                        pl.ds(pl.multiple_of(block * 16, 16), 16), :
                    ]
        for n in range(0, 768, 256):
            out_ref[:, n : n + 256] = jnp.dot(
                held[dc], back_ref[:, n : n + 256], preferred_element_type=F32
            ).astype(out_ref.dtype)


VMEM_SPEC = pl.BlockSpec(memory_space=pltpu.VMEM)
SMEM_SPEC = pl.BlockSpec(memory_space=pltpu.SMEM)


def call(kernel, name, outs, scratch, specs, *args):
    return pl.pallas_call(
        kernel,
        out_shape=outs,
        in_specs=specs,
        out_specs=jax.tree.map(lambda _: VMEM_SPEC, outs),
        scratch_shapes=scratch,
        compiler_params=pltpu.CompilerParams(vmem_limit_bytes=60 * 2**20),
        name=name,
    )(*args)


def array(shape, dtype):
    return jax.ShapeDtypeStruct(shape, dtype)


def on_device(
    latents, labels, slot_source, episode_pick, window_start, proj_weight, norm_gain, head_weight
):
    position = lax.axis_index("dp")
    c, xl, zl, zh = position % 2, (position // 2) % 2, (position // 4) % 4, position // 16
    pieces = cut_windows(
        latents, labels, slot_source, episode_pick, window_start, position, lax.axis_index("mp")
    )
    pieces = exchange(jnp.transpose(pieces, (1, 0, 2)), "dp")
    proj_own = gather(proj_weight, "dp", ZH_GROUPS)
    pieces, proj_own = tie(pieces, proj_own)
    proj_xlo = permute(proj_own, to_xlo)
    ordered = pieces.reshape(128, 640)[slot_source].reshape(PEERS, 2, 640)
    ordered, proj_own = tie(ordered, proj_own)
    arrived = exchange(ordered, "dp")
    proj_own = gather(jnp.concatenate([proj_own, proj_xlo]), "dp", ZL_GROUPS)
    proj_own = proj_own.reshape(4, 2, 4, 16, 768)
    arrived, proj_own = tie(arrived, proj_own)
    proj_core = permute(proj_own, to_core)
    gathered = exchange(order_rows(jnp.transpose(arrived, (1, 0, 2))), "mp")

    place = jnp.stack([xl, c])
    gain = norm_gain.reshape(1, 768)
    sent, hidden, inputs = call(
        forward_kernel,
        "forward",
        (array((8, SENT, 128), BF), array((ROWS, 768), F32), array((ROWS, 1024), BF)),
        [pltpu.VMEM((1024, 768), BF), pltpu.VMEM((ROWS, 768), BF)],
        [SMEM_SPEC] + [VMEM_SPEC] * 5,
        place, gathered, proj_own, proj_core, gain, head_weight,
    )
    all_sent = exchange(sent, "mp")
    features, back_hidden, head_rows = call(
        backward_kernel,
        "backward",
        (array((ROWS, 768), BF), array((ROWS, 768), BF), array((128, 896), BF)),
        [pltpu.VMEM((ROWS, 128), F32), pltpu.VMEM((ROWS, 128), BF), pltpu.VMEM((8, 768), F32)],
        [VMEM_SPEC] * 5,
        all_sent, gathered[:, 512:576], hidden, gain, head_weight,
    )
    kept, given = call(
        weight_kernel,
        "weight",
        (array((ROWS, 768), F32), array((ROWS, 768), BF)),
        [pltpu.VMEM((2, ROWS, ROWS), BF)],
        [SMEM_SPEC] + [VMEM_SPEC] * 2,
        place, jnp.transpose(inputs), back_hidden,
    )

    kept = kept + permute(given, to_core).astype(F32)
    head_rows, kept = tie(head_rows, kept)
    part = exchange(head_rows.reshape(16, 8, 896), "dp", Z_GROUPS)
    kept = kept[:256] + permute(kept[256:].astype(BF), to_xlo).astype(F32)
    blocks = kept.reshape(4, 64, 768)
    from_zl = [permute(take(blocks, (zl + k) % 4, 0).astype(BF), to_zl(k)) for k in (1, 2, 3)]
    part, first = tie(part, from_zl[0])
    part = jnp.sum(part.astype(F32), axis=0)
    part = part + permute(part, to_core)
    kept = take(blocks, zl, 0)
    for block in (first, from_zl[1], from_zl[2]):
        kept = kept + block.astype(F32)
    part = part + permute(part, to_xlo)
    grad_proj = exchange(kept.astype(BF).reshape(4, 16, 768), "dp", ZH_GROUPS)
    grad_proj = jnp.sum(grad_proj.astype(F32), axis=0)
    whole = gather(part, "dp", Z_GROUPS).reshape(16, 8, 896)
    grad_head = jnp.transpose(whole[:, :, :768].reshape(128, 768))
    grad_gain = whole[:, 0, 768:816].reshape(768)
    return (grad_proj, grad_head, grad_gain, features)


def solution(mesh):
    in_specs = (
        P("dp", None, "mp"),
        P("dp", None, None),
        P(),
        P(),
        P(),
        P("dp", "mp"),
        P("mp"),
        P("mp", None),
    )
    out_specs = (P("dp", "mp"), P("mp", None), P("mp"), P("dp", "mp"))
    return jax.shard_map(
        on_device, mesh=mesh, in_specs=in_specs, out_specs=out_specs, check_vma=False
    )
```

```python
import math

import jax
import jax.numpy as jnp
from jax import lax
from jax.experimental import pallas as pl
from jax.experimental.pallas import tpu as pltpu
from jax.sharding import PartitionSpec as P

D = 6144
WIN = 256
EPSILON = 1e-05
BF = jnp.bfloat16
F32 = jnp.float32

N_DP = 64
Z_GROUPS = [[z * 4 + q for z in range(16)] for q in range(4)]
ZH_GROUPS = [[zh * 16 + q for zh in range(4)] for q in range(16)]
ZL_GROUPS = [[zh * 16 + zl * 4 + q for zl in range(4)] for zh in range(4) for q in range(4)]


def to_core(i):
    return i ^ 1


def to_xlo(i):
    return i ^ 2


def to_zl(k):
    return lambda i: (i & ~12) | ((i + 4 * k) & 12)


def to_zh(k):
    return lambda i: (i + 16 * k) % N_DP


def permute(x, target):
    return lax.ppermute(x, "dp", [(i, target(i)) for i in range(N_DP)])


def exchange(x, axis, groups=None):
    return lax.all_to_all(
        x, axis, split_axis=0, concat_axis=0, tiled=True, axis_index_groups=groups
    )


def gather(x, axis, groups=None):
    return lax.all_gather(x, axis, axis=0, tiled=True, axis_index_groups=groups)


def copies(x, n):
    return jnp.broadcast_to(x[None], (n,) + x.shape)


def take(x, index, axis):
    return lax.dynamic_index_in_dim(x, index, axis, keepdims=False)


def pair(mine, other, index):
    return jnp.where(index == 0, jnp.stack([mine, other]), jnp.stack([other, mine]))


def tie(x, y):
    return lax.optimization_barrier((x, y))


PEERS = 64


def cut_kernel(
    position_ref, slot_ref, pick_ref, start_ref, latents_ref, labels_ref,
    pieces_ref, lat_held, lab_held, wide, sems,
):
    shifts, moves = [], []
    for k in range(2):
        here = slot_ref[...] == position_ref[0] * 2 + k
        episode = jnp.sum(jnp.where(here, pick_ref[...], 0).astype(F32)).astype(jnp.int32)
        start = jnp.sum(jnp.where(here, start_ref[...], 0).astype(F32)).astype(jnp.int32)
        first = pl.multiple_of(jnp.minimum(start // 16, 15) * 16, 16)
        shifts.append(start - first)
        for n, (store, held) in enumerate(((latents_ref, lat_held), (labels_ref, lab_held))):
            move = pltpu.make_async_copy(
                store.at[episode, pl.ds(first, WIN + 16), :], held.at[k], sems.at[n, k]
            )
            move.start()
            moves.append(move)
    part = position_ref[1]
    for k in range(2):
        moves[2 * k].wait()
        moves[2 * k + 1].wait()
        wide[0, : WIN + 16] = lat_held[k].astype(F32)
        wide[1, : WIN + 16] = lab_held[k].astype(F32)
        for r in range(4):
            rows = wide[0, pl.ds(shifts[k] + r, PEERS, stride=4), :]
            pieces_ref[k, :, r * 128 : (r + 1) * 128] = rows.astype(BF)
        rows = wide[1, pl.ds(shifts[k] + part // 2, PEERS, stride=4), :]
        rows = jnp.where(part % 2 == 0, rows, pltpu.roll(rows, 64, 1))
        pieces_ref[k, :, 512:640] = rows.astype(BF)


def cut_windows(latents, labels, slot_source, episode_pick, window_start, position, part):
    smem = pl.BlockSpec(memory_space=pltpu.SMEM)
    vmem = pl.BlockSpec(memory_space=pltpu.VMEM)
    hbm = pl.BlockSpec(memory_space=pltpu.HBM)
    return pl.pallas_call(
        cut_kernel,
        out_shape=jax.ShapeDtypeStruct((2, PEERS, 640), BF),
        in_specs=[smem, vmem, vmem, vmem, hbm, hbm],
        out_specs=vmem,
        scratch_shapes=[
            pltpu.VMEM((2, WIN + 16, 128), BF),
            pltpu.VMEM((2, WIN + 16, 128), BF),
            pltpu.VMEM((2, WIN + 24, 128), F32),
            pltpu.SemaphoreType.DMA((2, 2)),
        ],
        compiler_params=pltpu.CompilerParams(vmem_limit_bytes=60 * 2**20),
        name="cut_windows",
    )(
        jnp.stack([position, part]),
        slot_source.reshape(1, 128),
        episode_pick.reshape(1, 128),
        window_start.reshape(1, 128),
        latents,
        labels,
    )


def order_kernel(arrived_ref, copies_ref, wide):
    for w in range(2):
        for r in range(4):
            wide[pl.ds(w * WIN + r, PEERS, stride=4), :] = arrived_ref[
                w, :, r * 128 : (r + 1) * 128
            ].astype(F32)
    first = arrived_ref[0, :, 512:640].astype(F32)
    second = pltpu.roll(arrived_ref[1, :, 512:640].astype(F32), 64, 1)
    lane = lax.broadcasted_iota(jnp.int32, (PEERS, 128), 1)
    both = jnp.where(lane < 64, first, second).astype(BF)
    rows = wide[...].astype(BF)
    for m in range(8):
        copies_ref[m, :512, :] = rows
        copies_ref[m, 512:576, :] = both
        copies_ref[m, 576:640, :] = jnp.zeros((64, 128), BF)


def order_rows(arrived):
    vmem = pl.BlockSpec(memory_space=pltpu.VMEM)
    return pl.pallas_call(
        order_kernel,
        out_shape=jax.ShapeDtypeStruct((8, 640, 128), BF),
        in_specs=[vmem],
        out_specs=vmem,
        scratch_shapes=[pltpu.VMEM((512, 128), F32)],
        compiler_params=pltpu.CompilerParams(vmem_limit_bytes=60 * 2**20),
        name="order_rows",
    )(arrived)


CHUNK = 128
ROWS = 512
SENT = 640


def two_parts(x):
    high = x.astype(BF).astype(F32)
    return high, x - high


def forward_kernel(
    place_ref, gathered_ref, own_ref, core_ref, gain_ref, head_ref,
    sent_ref, hidden_ref, inputs_ref, proj, scaled,
):
    xl, c = place_ref[0], place_ref[1]
    for zl in range(4):
        for zh in range(4):
            for dx in range(2):
                for dc, ref in enumerate((own_ref, core_ref)):
                    block = (zh * 4 + zl) * 4 + (xl ^ dx) * 2 + (c ^ dc)
                    proj[pl.ds(pl.multiple_of(block * 16, 16), 16), :] = ref[zl, dx, zh]
    for m in range(8):
        inputs_ref[:, m * 128 : (m + 1) * 128] = gathered_ref[m, :ROWS, :]
    gain = gain_ref[...]
    lane = lax.broadcasted_iota(jnp.int32, (CHUNK, 128), 1)
    row = lax.broadcasted_iota(jnp.int32, (16, 768), 0)
    gain_high, rest = two_parts(gain)
    gain_mid, gain_low = two_parts(rest)
    gains = jnp.where(
        row == 0, gain_high, jnp.where(row == 1, gain_mid, jnp.where(row == 2, gain_low, 0.0))
    )
    gain_head = jnp.sum(
        jnp.dot(gains.astype(BF), head_ref[...], preferred_element_type=F32), axis=0, keepdims=True
    )
    high, rest = two_parts(gain_head)
    mid, low = two_parts(rest)
    row = lax.broadcasted_iota(jnp.int32, (16, 128), 0)
    gain_head = jnp.where(row == 0, high, jnp.where(row == 1, mid, jnp.where(row == 2, low, 0.0)))
    for m in range(8):
        sent_ref[m, 576:592, :] = gain_head.astype(BF)
        sent_ref[m, 592:640, :] = jnp.zeros((48, 128), BF)

    for n in range(0, 768, 256):
        hidden_ref[:, n : n + 256] = jnp.dot(
            inputs_ref[...], proj[:, n : n + 256], preferred_element_type=F32
        )
    for i in range(0, ROWS, CHUNK):
        hidden = hidden_ref[i : i + CHUNK, :]
        mean = jnp.sum(hidden, axis=1, keepdims=True) / 768
        centred = hidden - mean
        square = jnp.sum(centred * centred, axis=1, keepdims=True)
        scaled[i : i + CHUNK, :] = (centred * gain).astype(BF)
        parts = []
        for value in (mean, square):
            high, rest = two_parts(value)
            mid, low = two_parts(rest)
            parts += [high, mid, low]
        packed = jnp.zeros((CHUNK, 128), F32)
        for k, value in enumerate(parts):
            packed = jnp.where(lane == k, value, packed)
        packed = packed.T[:16].astype(BF)
        start = ROWS + i // 8
        for m in range(8):
            sent_ref[m, start : start + 16, :] = packed
    partial = jnp.dot(scaled[...], head_ref[...], preferred_element_type=F32).astype(BF)
    for m in range(8):
        sent_ref[m, :ROWS, :] = partial


def backward_kernel(
    sent_ref, labels_ref, hidden_ref, gain_ref, head_ref,
    features_ref, back_ref, head_rows_ref, targets, errors, gain_sum,
):
    gain = gain_ref[...]
    lane = lax.broadcasted_iota(jnp.int32, (64, 128), 1)
    for r in range(4):
        one = labels_ref[2 * r].astype(F32)
        two = labels_ref[2 * r + 1].astype(F32)
        targets[pl.ds(r, 64, stride=4), :] = jnp.where(lane < 64, one, pltpu.roll(two, 64, 1))
        targets[pl.ds(WIN + r, 64, stride=4), :] = jnp.where(
            lane < 64, pltpu.roll(one, 64, 1), two
        )
    gain_heads = [
        jnp.sum(sent_ref[m, 576:592, :].astype(F32), axis=0, keepdims=True) for m in range(8)
    ]
    gain_head = sum(gain_heads)
    gain_sum[...] = jnp.zeros((8, 768), F32)

    for i in range(ROWS // CHUNK):
        rows = slice(i * CHUNK, (i + 1) * CHUNK)
        start = ROWS + i * 16
        stats = [sent_ref[m, start : start + 16, :].astype(F32) for m in range(8)]
        means = [part[0:1] + part[1:2] + part[2:3] for part in stats]
        mean = sum(means) / 8
        offs = [value - mean for value in means]
        squares = sum(part[3:4] + part[4:5] + part[5:6] for part in stats)
        squares += 768 * sum(off * off for off in offs)
        scale = lax.rsqrt(squares / D + EPSILON)
        turned = jnp.concatenate(offs + [mean, scale, jnp.zeros((118, 128), F32)], axis=0).T
        mean, scale = turned[:, 8:9], turned[:, 9:10]
        summed = sent_ref[0, rows, :].astype(F32)
        for m in range(1, 8):
            summed += sent_ref[m, rows, :].astype(F32)
        for m in range(8):
            summed += turned[:, m : m + 1] * gain_heads[m]
        predicted = scale * summed
        error = ((predicted - targets[rows, :]) / math.sqrt(32768)).astype(BF)
        errors[rows, :] = error
        wide = error.astype(F32)
        first = jnp.sum(wide * gain_head, axis=1, keepdims=True) / D
        second = jnp.sum(wide * predicted, axis=1, keepdims=True) / D
        normed = (hidden_ref[rows, :] - mean) * scale
        features_ref[rows, :] = (normed * gain).astype(BF)
        back = lax.dot_general(
            error, head_ref[...], (((1,), (1,)), ((), ())), preferred_element_type=F32
        )
        gain_sum[...] += jnp.sum((back * normed).reshape(CHUNK // 8, 8, 768), axis=0)
        back_ref[rows, :] = (scale * (back * gain - first - normed * second)).astype(BF)

    head_rows_ref[:, :768] = lax.dot_general(
        errors[...], features_ref[...], (((0,), (0,)), ((), ())), preferred_element_type=F32
    ).astype(BF)
    total = jnp.broadcast_to(jnp.sum(gain_sum[...], axis=0, keepdims=True), (8, 768))
    place = lax.broadcasted_iota(jnp.int32, (8, 128), 0)
    lane = lax.broadcasted_iota(jnp.int32, (8, 128), 1)
    for z in range(0, 16, 2):
        pair_rows = []
        for y in (z, z + 1):
            turned = total if y == 0 else pltpu.roll(total, 768 - 48 * y, 1)
            pair_rows.append(jnp.where((place == 0) & (lane < 48), turned[:, :128], 0.0))
        head_rows_ref[z * 8 : z * 8 + 16, 768:] = jnp.concatenate(pair_rows, axis=0).astype(BF)


def weight_kernel(place_ref, turned_ref, back_ref, kept_ref, given_ref, held):
    xl, c = place_ref[0], place_ref[1]
    for dc, out_ref in enumerate((kept_ref, given_ref)):
        for dx in range(2):
            for zl in range(4):
                for zh in range(4):
                    block = ((zh * 4 + zl) * 2 + (xl ^ dx)) * 2 + (c ^ dc)
                    row = dx * 256 + (zh * 4 + zl) * 16
                    held[dc, row : row + 16, :] = turned_ref[
                        pl.ds(pl.multiple_of(block * 16, 16), 16), :
                    ]
        for n in range(0, 768, 256):
            out_ref[:, n : n + 256] = jnp.dot(
                held[dc], back_ref[:, n : n + 256], preferred_element_type=F32
            ).astype(out_ref.dtype)


VMEM_SPEC = pl.BlockSpec(memory_space=pltpu.VMEM)
SMEM_SPEC = pl.BlockSpec(memory_space=pltpu.SMEM)


def call(kernel, name, outs, scratch, specs, *args):
    return pl.pallas_call(
        kernel,
        out_shape=outs,
        in_specs=specs,
        out_specs=jax.tree.map(lambda _: VMEM_SPEC, outs),
        scratch_shapes=scratch,
        compiler_params=pltpu.CompilerParams(vmem_limit_bytes=60 * 2**20),
        name=name,
    )(*args)


def array(shape, dtype):
    return jax.ShapeDtypeStruct(shape, dtype)


def on_device(
    latents, labels, slot_source, episode_pick, window_start, proj_weight, norm_gain, head_weight
):
    position = lax.axis_index("dp")
    c, xl, zl, zh = position % 2, (position // 2) % 2, (position // 4) % 4, position // 16
    pieces = cut_windows(
        latents, labels, slot_source, episode_pick, window_start, position, lax.axis_index("mp")
    )
    pieces = exchange(jnp.transpose(pieces, (1, 0, 2)), "dp")
    proj_own = gather(proj_weight, "dp", ZH_GROUPS)
    pieces, proj_own = tie(pieces, proj_own)
    proj_xlo = permute(proj_own, to_xlo)
    ordered = pieces.reshape(128, 640)[slot_source].reshape(PEERS, 2, 640)
    ordered, proj_own = tie(ordered, proj_own)
    arrived = exchange(ordered, "dp")
    proj_own = gather(jnp.concatenate([proj_own, proj_xlo]), "dp", ZL_GROUPS)
    proj_own = proj_own.reshape(4, 2, 4, 16, 768)
    arrived, proj_own = tie(arrived, proj_own)
    proj_core = permute(proj_own, to_core)
    gathered = exchange(order_rows(jnp.transpose(arrived, (1, 0, 2))), "mp")

    place = jnp.stack([xl, c])
    gain = norm_gain.reshape(1, 768)
    sent, hidden, inputs = call(
        forward_kernel,
        "forward",
        (array((8, SENT, 128), BF), array((ROWS, 768), F32), array((ROWS, 1024), BF)),
        [pltpu.VMEM((1024, 768), BF), pltpu.VMEM((ROWS, 768), BF)],
        [SMEM_SPEC] + [VMEM_SPEC] * 5,
        place, gathered, proj_own, proj_core, gain, head_weight,
    )
    all_sent = exchange(sent, "mp")
    features, back_hidden, head_rows = call(
        backward_kernel,
        "backward",
        (array((ROWS, 768), BF), array((ROWS, 768), BF), array((128, 896), BF)),
        [pltpu.VMEM((ROWS, 128), F32), pltpu.VMEM((ROWS, 128), BF), pltpu.VMEM((8, 768), F32)],
        [VMEM_SPEC] * 5,
        all_sent, gathered[:, 512:576], hidden, gain, head_weight,
    )
    kept, given = call(
        weight_kernel,
        "weight",
        (array((ROWS, 768), F32), array((ROWS, 768), BF)),
        [pltpu.VMEM((2, ROWS, ROWS), BF)],
        [SMEM_SPEC] + [VMEM_SPEC] * 2,
        place, jnp.transpose(inputs), back_hidden,
    )

    kept = kept + permute(given, to_core).astype(F32)
    head_rows, kept = tie(head_rows, kept)
    part = exchange(head_rows.reshape(16, 8, 896), "dp", Z_GROUPS)
    kept = kept[:256] + permute(kept[256:].astype(BF), to_xlo).astype(F32)
    part, kept = tie(part, kept)
    grad_proj = exchange(kept.astype(BF).reshape(16, 16, 768), "dp", Z_GROUPS)
    grad_proj = jnp.sum(grad_proj.astype(F32), axis=0)
    part = jnp.sum(part.astype(F32), axis=0)
    part = part + permute(part, to_core)
    part = part + permute(part, to_xlo)
    whole = gather(part, "dp", Z_GROUPS).reshape(16, 8, 896)
    grad_head = jnp.transpose(whole[:, :, :768].reshape(128, 768))
    grad_gain = whole[:, 0, 768:816].reshape(768)
    return (grad_proj, grad_head, grad_gain, features)


def solution(mesh):
    in_specs = (
        P("dp", None, "mp"),
        P("dp", None, None),
        P(),
        P(),
        P(),
        P("dp", "mp"),
        P("mp"),
        P("mp", None),
    )
    out_specs = (P("dp", "mp"), P("mp", None), P("mp"), P("dp", "mp"))
    return jax.shard_map(
        on_device, mesh=mesh, in_specs=in_specs, out_specs=out_specs, check_vma=False
    )
```

```python
import math

import jax
import jax.numpy as jnp
from jax import lax
from jax.experimental import pallas as pl
from jax.experimental.pallas import tpu as pltpu
from jax.sharding import PartitionSpec as P

D = 6144
WIN = 256
EPSILON = 1e-05
BF = jnp.bfloat16
F32 = jnp.float32

N_DP = 64
Z_GROUPS = [[z * 4 + q for z in range(16)] for q in range(4)]
ZH_GROUPS = [[zh * 16 + q for zh in range(4)] for q in range(16)]
ZL_GROUPS = [[zh * 16 + zl * 4 + q for zl in range(4)] for zh in range(4) for q in range(4)]


def to_core(i):
    return i ^ 1


def to_xlo(i):
    return i ^ 2


def to_zl(k):
    return lambda i: (i & ~12) | ((i + 4 * k) & 12)


def to_zh(k):
    return lambda i: (i + 16 * k) % N_DP


def permute(x, target):
    return lax.ppermute(x, "dp", [(i, target(i)) for i in range(N_DP)])


def exchange(x, axis, groups=None):
    return lax.all_to_all(
        x, axis, split_axis=0, concat_axis=0, tiled=True, axis_index_groups=groups
    )


def gather(x, axis, groups=None):
    return lax.all_gather(x, axis, axis=0, tiled=True, axis_index_groups=groups)


def copies(x, n):
    return jnp.broadcast_to(x[None], (n,) + x.shape)


def take(x, index, axis):
    return lax.dynamic_index_in_dim(x, index, axis, keepdims=False)


def pair(mine, other, index):
    return jnp.where(index == 0, jnp.stack([mine, other]), jnp.stack([other, mine]))


def tie(x, y):
    return lax.optimization_barrier((x, y))


PEERS = 64


def cut_kernel(
    position_ref, slot_ref, pick_ref, start_ref, latents_ref, labels_ref,
    pieces_ref, lat_held, lab_held, wide, sems,
):
    shifts, moves = [], []
    for k in range(2):
        here = slot_ref[...] == position_ref[0] * 2 + k
        episode = jnp.sum(jnp.where(here, pick_ref[...], 0).astype(F32)).astype(jnp.int32)
        start = jnp.sum(jnp.where(here, start_ref[...], 0).astype(F32)).astype(jnp.int32)
        first = pl.multiple_of(jnp.minimum(start // 16, 15) * 16, 16)
        shifts.append(start - first)
        for n, (store, held) in enumerate(((latents_ref, lat_held), (labels_ref, lab_held))):
            move = pltpu.make_async_copy(
                store.at[episode, pl.ds(first, WIN + 16), :], held.at[k], sems.at[n, k]
            )
            move.start()
            moves.append(move)
    part = position_ref[1]
    for k in range(2):
        moves[2 * k].wait()
        moves[2 * k + 1].wait()
        wide[0, : WIN + 16] = lat_held[k].astype(F32)
        wide[1, : WIN + 16] = lab_held[k].astype(F32)
        for r in range(4):
            rows = wide[0, pl.ds(shifts[k] + r, PEERS, stride=4), :]
            pieces_ref[k, :, r * 128 : (r + 1) * 128] = rows.astype(BF)
        rows = wide[1, pl.ds(shifts[k] + part // 2, PEERS, stride=4), :]
        rows = jnp.where(part % 2 == 0, rows, pltpu.roll(rows, 64, 1))
        pieces_ref[k, :, 512:640] = rows.astype(BF)


def cut_windows(latents, labels, slot_source, episode_pick, window_start, position, part):
    smem = pl.BlockSpec(memory_space=pltpu.SMEM)
    vmem = pl.BlockSpec(memory_space=pltpu.VMEM)
    hbm = pl.BlockSpec(memory_space=pltpu.HBM)
    return pl.pallas_call(
        cut_kernel,
        out_shape=jax.ShapeDtypeStruct((2, PEERS, 640), BF),
        in_specs=[smem, vmem, vmem, vmem, hbm, hbm],
        out_specs=vmem,
        scratch_shapes=[
            pltpu.VMEM((2, WIN + 16, 128), BF),
            pltpu.VMEM((2, WIN + 16, 128), BF),
            pltpu.VMEM((2, WIN + 24, 128), F32),
            pltpu.SemaphoreType.DMA((2, 2)),
        ],
        compiler_params=pltpu.CompilerParams(vmem_limit_bytes=60 * 2**20),
        name="cut_windows",
    )(
        jnp.stack([position, part]),
        slot_source.reshape(1, 128),
        episode_pick.reshape(1, 128),
        window_start.reshape(1, 128),
        latents,
        labels,
    )


def order_kernel(arrived_ref, copies_ref, wide):
    for w in range(2):
        for r in range(4):
            wide[pl.ds(w * WIN + r, PEERS, stride=4), :] = arrived_ref[
                w, :, r * 128 : (r + 1) * 128
            ].astype(F32)
    first = arrived_ref[0, :, 512:640].astype(F32)
    second = pltpu.roll(arrived_ref[1, :, 512:640].astype(F32), 64, 1)
    lane = lax.broadcasted_iota(jnp.int32, (PEERS, 128), 1)
    both = jnp.where(lane < 64, first, second).astype(BF)
    rows = wide[...].astype(BF)
    for m in range(8):
        copies_ref[m, :512, :] = rows
        copies_ref[m, 512:576, :] = both
        copies_ref[m, 576:640, :] = jnp.zeros((64, 128), BF)


def order_rows(arrived):
    vmem = pl.BlockSpec(memory_space=pltpu.VMEM)
    return pl.pallas_call(
        order_kernel,
        out_shape=jax.ShapeDtypeStruct((8, 640, 128), BF),
        in_specs=[vmem],
        out_specs=vmem,
        scratch_shapes=[pltpu.VMEM((512, 128), F32)],
        compiler_params=pltpu.CompilerParams(vmem_limit_bytes=60 * 2**20),
        name="order_rows",
    )(arrived)


CHUNK = 128
ROWS = 512
SENT = 640


def two_parts(x):
    high = x.astype(BF).astype(F32)
    return high, x - high


def forward_kernel(
    place_ref, gathered_ref, own_ref, core_ref, gain_ref, head_ref,
    sent_ref, hidden_ref, inputs_ref, proj, scaled,
):
    xl, c = place_ref[0], place_ref[1]
    for zl in range(4):
        for zh in range(4):
            for dx in range(2):
                for dc, ref in enumerate((own_ref, core_ref)):
                    block = (zh * 4 + zl) * 4 + (xl ^ dx) * 2 + (c ^ dc)
                    proj[pl.ds(pl.multiple_of(block * 16, 16), 16), :] = ref[zl, dx, zh]
    for m in range(8):
        inputs_ref[:, m * 128 : (m + 1) * 128] = gathered_ref[m, :ROWS, :]
    gain = gain_ref[...]
    lane = lax.broadcasted_iota(jnp.int32, (CHUNK, 128), 1)
    row = lax.broadcasted_iota(jnp.int32, (16, 768), 0)
    gain_high, rest = two_parts(gain)
    gain_mid, gain_low = two_parts(rest)
    gains = jnp.where(
        row == 0, gain_high, jnp.where(row == 1, gain_mid, jnp.where(row == 2, gain_low, 0.0))
    )
    gain_head = jnp.sum(
        jnp.dot(gains.astype(BF), head_ref[...], preferred_element_type=F32), axis=0, keepdims=True
    )
    high, rest = two_parts(gain_head)
    mid, low = two_parts(rest)
    row = lax.broadcasted_iota(jnp.int32, (16, 128), 0)
    gain_head = jnp.where(row == 0, high, jnp.where(row == 1, mid, jnp.where(row == 2, low, 0.0)))
    for m in range(8):
        sent_ref[m, 576:592, :] = gain_head.astype(BF)
        sent_ref[m, 592:640, :] = jnp.zeros((48, 128), BF)

    for n in range(0, 768, 256):
        hidden_ref[:, n : n + 256] = jnp.dot(
            inputs_ref[...], proj[:, n : n + 256], preferred_element_type=F32
        )
    for i in range(0, ROWS, CHUNK):
        hidden = hidden_ref[i : i + CHUNK, :]
        mean = jnp.sum(hidden, axis=1, keepdims=True) / 768
        centred = hidden - mean
        square = jnp.sum(centred * centred, axis=1, keepdims=True)
        scaled[i : i + CHUNK, :] = (centred * gain).astype(BF)
        parts = []
        for value in (mean, square):
            high, rest = two_parts(value)
            mid, low = two_parts(rest)
            parts += [high, mid, low]
        packed = jnp.zeros((CHUNK, 128), F32)
        for k, value in enumerate(parts):
            packed = jnp.where(lane == k, value, packed)
        packed = packed.T[:16].astype(BF)
        start = ROWS + i // 8
        for m in range(8):
            sent_ref[m, start : start + 16, :] = packed
    partial = jnp.dot(scaled[...], head_ref[...], preferred_element_type=F32).astype(BF)
    for m in range(8):
        sent_ref[m, :ROWS, :] = partial


def backward_kernel(
    sent_ref, labels_ref, hidden_ref, gain_ref, head_ref,
    features_ref, back_ref, head_rows_ref, targets, errors, gain_sum,
):
    gain = gain_ref[...]
    lane = lax.broadcasted_iota(jnp.int32, (64, 128), 1)
    for r in range(4):
        one = labels_ref[2 * r].astype(F32)
        two = labels_ref[2 * r + 1].astype(F32)
        targets[pl.ds(r, 64, stride=4), :] = jnp.where(lane < 64, one, pltpu.roll(two, 64, 1))
        targets[pl.ds(WIN + r, 64, stride=4), :] = jnp.where(
            lane < 64, pltpu.roll(one, 64, 1), two
        )
    gain_heads = [
        jnp.sum(sent_ref[m, 576:592, :].astype(F32), axis=0, keepdims=True) for m in range(8)
    ]
    gain_head = sum(gain_heads)
    gain_sum[...] = jnp.zeros((8, 768), F32)

    for i in range(ROWS // CHUNK):
        rows = slice(i * CHUNK, (i + 1) * CHUNK)
        start = ROWS + i * 16
        stats = [sent_ref[m, start : start + 16, :].astype(F32) for m in range(8)]
        means = [part[0:1] + part[1:2] + part[2:3] for part in stats]
        mean = sum(means) / 8
        offs = [value - mean for value in means]
        squares = sum(part[3:4] + part[4:5] + part[5:6] for part in stats)
        squares += 768 * sum(off * off for off in offs)
        scale = lax.rsqrt(squares / D + EPSILON)
        turned = jnp.concatenate(offs + [mean, scale, jnp.zeros((118, 128), F32)], axis=0).T
        mean, scale = turned[:, 8:9], turned[:, 9:10]
        summed = sent_ref[0, rows, :].astype(F32)
        for m in range(1, 8):
            summed += sent_ref[m, rows, :].astype(F32)
        for m in range(8):
            summed += turned[:, m : m + 1] * gain_heads[m]
        predicted = scale * summed
        error = ((predicted - targets[rows, :]) / math.sqrt(32768)).astype(BF)
        errors[rows, :] = error
        wide = error.astype(F32)
        first = jnp.sum(wide * gain_head, axis=1, keepdims=True) / D
        second = jnp.sum(wide * predicted, axis=1, keepdims=True) / D
        normed = (hidden_ref[rows, :] - mean) * scale
        features_ref[rows, :] = (normed * gain).astype(BF)
        back = lax.dot_general(
            error, head_ref[...], (((1,), (1,)), ((), ())), preferred_element_type=F32
        )
        gain_sum[...] += jnp.sum((back * normed).reshape(CHUNK // 8, 8, 768), axis=0)
        back_ref[rows, :] = (scale * (back * gain - first - normed * second)).astype(BF)

    head_rows_ref[:, :768] = lax.dot_general(
        errors[...], features_ref[...], (((0,), (0,)), ((), ())), preferred_element_type=F32
    ).astype(BF)
    total = jnp.broadcast_to(jnp.sum(gain_sum[...], axis=0, keepdims=True), (8, 768))
    place = lax.broadcasted_iota(jnp.int32, (8, 128), 0)
    lane = lax.broadcasted_iota(jnp.int32, (8, 128), 1)
    for z in range(0, 16, 2):
        pair_rows = []
        for y in (z, z + 1):
            turned = total if y == 0 else pltpu.roll(total, 768 - 48 * y, 1)
            pair_rows.append(jnp.where((place == 0) & (lane < 48), turned[:, :128], 0.0))
        head_rows_ref[z * 8 : z * 8 + 16, 768:] = jnp.concatenate(pair_rows, axis=0).astype(BF)


def weight_kernel(place_ref, turned_ref, back_ref, kept_ref, given_ref, held):
    xl, c = place_ref[0], place_ref[1]
    for dc, out_ref in enumerate((kept_ref, given_ref)):
        for dx in range(2):
            for zl in range(4):
                for zh in range(4):
                    block = ((zh * 4 + zl) * 2 + (xl ^ dx)) * 2 + (c ^ dc)
                    row = dx * 256 + (zh * 4 + zl) * 16
                    held[dc, row : row + 16, :] = turned_ref[
                        pl.ds(pl.multiple_of(block * 16, 16), 16), :
                    ]
        for n in range(0, 768, 256):
            out_ref[:, n : n + 256] = jnp.dot(
                held[dc], back_ref[:, n : n + 256], preferred_element_type=F32
            ).astype(out_ref.dtype)


VMEM_SPEC = pl.BlockSpec(memory_space=pltpu.VMEM)
SMEM_SPEC = pl.BlockSpec(memory_space=pltpu.SMEM)


def call(kernel, name, outs, scratch, specs, *args):
    return pl.pallas_call(
        kernel,
        out_shape=outs,
        in_specs=specs,
        out_specs=jax.tree.map(lambda _: VMEM_SPEC, outs),
        scratch_shapes=scratch,
        compiler_params=pltpu.CompilerParams(vmem_limit_bytes=60 * 2**20),
        name=name,
    )(*args)


def array(shape, dtype):
    return jax.ShapeDtypeStruct(shape, dtype)


def on_device(
    latents, labels, slot_source, episode_pick, window_start, proj_weight, norm_gain, head_weight
):
    position = lax.axis_index("dp")
    c, xl, zl, zh = position % 2, (position // 2) % 2, (position // 4) % 4, position // 16
    pieces = cut_windows(
        latents, labels, slot_source, episode_pick, window_start, position, lax.axis_index("mp")
    )
    pieces = exchange(jnp.transpose(pieces, (1, 0, 2)), "dp")
    proj_own = gather(proj_weight, "dp", ZH_GROUPS)
    pieces, proj_own = tie(pieces, proj_own)
    proj_xlo = permute(proj_own, to_xlo)
    ordered = pieces.reshape(128, 640)[slot_source].reshape(PEERS, 2, 640)
    ordered, proj_own = tie(ordered, proj_own)
    arrived = exchange(ordered, "dp")
    proj_own = gather(jnp.concatenate([proj_own, proj_xlo]), "dp", ZL_GROUPS)
    proj_own = proj_own.reshape(4, 2, 4, 16, 768)
    arrived, proj_own = tie(arrived, proj_own)
    proj_core = permute(proj_own, to_core)
    gathered = exchange(order_rows(jnp.transpose(arrived, (1, 0, 2))), "mp")

    place = jnp.stack([xl, c])
    gain = norm_gain.reshape(1, 768)
    sent, hidden, inputs = call(
        forward_kernel,
        "forward",
        (array((8, SENT, 128), BF), array((ROWS, 768), F32), array((ROWS, 1024), BF)),
        [pltpu.VMEM((1024, 768), BF), pltpu.VMEM((ROWS, 768), BF)],
        [SMEM_SPEC] + [VMEM_SPEC] * 5,
        place, gathered, proj_own, proj_core, gain, head_weight,
    )
    all_sent = exchange(sent, "mp")
    features, back_hidden, head_rows = call(
        backward_kernel,
        "backward",
        (array((ROWS, 768), BF), array((ROWS, 768), BF), array((128, 896), BF)),
        [pltpu.VMEM((ROWS, 128), F32), pltpu.VMEM((ROWS, 128), BF), pltpu.VMEM((8, 768), F32)],
        [VMEM_SPEC] * 5,
        all_sent, gathered[:, 512:576], hidden, gain, head_weight,
    )
    kept, given = call(
        weight_kernel,
        "weight",
        (array((ROWS, 768), F32), array((ROWS, 768), BF)),
        [pltpu.VMEM((2, ROWS, ROWS), BF)],
        [SMEM_SPEC] + [VMEM_SPEC] * 2,
        place, jnp.transpose(inputs), back_hidden,
    )

    kept = kept + permute(given, to_core).astype(F32)
    head_rows, kept = tie(head_rows, kept)
    part = exchange(head_rows.reshape(16, 8, 896), "dp", Z_GROUPS)
    kept = kept[:256] + permute(kept[256:].astype(BF), to_xlo).astype(F32)
    part, kept = tie(part, kept)
    grad_proj = exchange(kept.astype(BF).reshape(16, 16, 768), "dp", Z_GROUPS)
    grad_proj = jnp.sum(grad_proj.astype(F32), axis=0)
    part = jnp.sum(part.astype(F32), axis=0)
    part = part + permute(part, to_core)
    part = part + permute(part, to_xlo)
    whole = gather(part.astype(BF), "dp", Z_GROUPS).reshape(16, 8, 896).astype(F32)
    grad_head = jnp.transpose(whole[:, :, :768].reshape(128, 768))
    grad_gain = whole[:, 0, 768:816].reshape(768)
    return (grad_proj, grad_head, grad_gain, features)


def solution(mesh):
    in_specs = (
        P("dp", None, "mp"),
        P("dp", None, None),
        P(),
        P(),
        P(),
        P("dp", "mp"),
        P("mp"),
        P("mp", None),
    )
    out_specs = (P("dp", "mp"), P("mp", None), P("mp"), P("dp", "mp"))
    return jax.shard_map(
        on_device, mesh=mesh, in_specs=in_specs, out_specs=out_specs, check_vma=False
    )
```
